32 devices in a mesh: ep: 4 (over y, x), fsdp: 8 (over z, core).
Axes of the slice: x: 2, y: 2, z: 4, core: 2. Of those that a mesh axis runs over, the one named last changes fastest.
Arguments:
- tokens: bfloat16 [512, 6144], P('ep', 'fsdp'), may hold values from -6 to 6
- expert_ids: int32 [512, 2], P('ep'), may hold values from 0 to 3, all different within a row; in each aligned block of 128 rows (0 to 127, 128 to 255, ...) at most 128 rows name the same one
- combine_weights: float32 [512, 2], P('ep'), may hold values from 0.25 to 1
- w_gate: bfloat16 [4, 6144, 8192], P('ep', None, 'fsdp'), may hold values from -0.078125 to 0.078125
- w_up: bfloat16 [4, 6144, 8192], P('ep', None, 'fsdp'), may hold values from -0.078125 to 0.078125
- w_down: bfloat16 [4, 8192, 6144], P('ep', 'fsdp'), may hold values from -0.0625 to 0.0625
Outputs:
- mixed_rows: bfloat16 [512, 6144], P('ep', 'fsdp')
The draws below stay inside these ranges and needn't reach their ends.
Inputs may be any that keep to these rules, and one draw needn't show every extreme that they name: `expert_ids`: among the 128 tokens of one index of ep (aligned blocks of rows), no expert is named by more than 128 rows, a bound that some block reaches; a token names two different experts.
All inputs are finite; a program needn't handle non-finite values.
Results may differ from the reference program's by a relative error of at most 0.0057.
Values may be sent and summed in bfloat16 or wider, within the bound.
A program may use at most 128 MiB of HBM per device.

```python
import math
import jax
import jax.numpy as jnp
import numpy as np
from jax import lax

D = 6144
FF = 8192
TOP = 2
TOK_EP = 128
EXPERTS = 4
CAP = 128
TOKENS = 512
N_EP = 4


def block_levels(stream_key, shape, shards, least, high):
    loudness = 1.0
    for axis_at, parts in shards:
        heights = jax.random.uniform(jax.random.fold_in(jax.random.fold_in(stream_key, 6), axis_at), (parts,), jnp.float32, least / len(shards), high / len(shards))
        loudness = loudness * jnp.repeat(jnp.exp(heights), shape[axis_at] // parts).reshape((-1,) + (1,) * (len(shape) - 1 - axis_at))
    return loudness


def shared_out(rng, own, number, rows, number_of, top, reach, slope):
    order = jax.random.permutation(rng, number_of)
    heavy_load, common = portions_of(number_of, rows * top, reach, slope, True), portions_of(number_of, rows * top, reach, slope, False)
    places = jnp.arange(number_of)

    def named(lengths, rotation):
        used = int((lengths > 0).sum())
        fixed = max(1, used // 4)
        passed = fixed + (places - fixed + rotation * (used - fixed)) % max(1, number_of - fixed)
        return jnp.zeros((number_of,), jnp.int32).at[order[jnp.where(places < fixed, places, passed)]].set(jnp.asarray(lengths, jnp.int32))

    lengths = jnp.where(number % 4 == 0, named(heavy_load, number // 4), named(common, number - number // 4 - 1))
    mixed = jax.random.permutation(jax.random.fold_in(own, 3), number_of)
    source_of, receiver = mixed[0:number_of // 2 * 2:2], mixed[1:number_of // 2 * 2:2]
    room = jnp.minimum(lengths[source_of] - 1, reach - lengths[receiver]) // 2
    room = jnp.where((source_of == order[0]) | (receiver == order[0]) | (lengths[receiver] == 0), 0, jnp.maximum(room, 0))
    passed = jax.random.randint(jax.random.fold_in(own, 4), (number_of // 2,), 0, 1 << 20) % (room + 1)
    lengths = lengths.at[source_of].add(-passed).at[receiver].add(passed)
    labels = jnp.searchsorted(jnp.cumsum(lengths), jnp.arange(rows * top), side="right").astype(jnp.int32)
    listing = labels.reshape(top, rows).T
    listing = listing[jax.random.permutation(jax.random.fold_in(own, 1), rows)]
    rotation = jax.random.randint(jax.random.fold_in(own, 2), (rows, 1), 0, top)
    return jnp.take_along_axis(listing, (jnp.arange(top)[None, :] + rotation) % top, axis=1)


def portions_of(number_of, total, most, skew, full):
    portions = [(1 << 20) // math.isqrt(rank ** skew) + 1 for rank in range(1, number_of + 1)]
    largest = most if full else min(most, max(-(-total // number_of), total * portions[0] // sum(portions)))
    least = 1 if total - largest >= number_of - 1 else 0
    counts, spare = [largest] + [least] * (number_of - 1), total - largest - least * (number_of - 1)
    while spare > 0:
        candidates = [i for i in range(1, number_of) if counts[i] < largest] or [i for i in range(1, number_of) if counts[i] < most]
        pool, remaining = sum([portions[i] for i in candidates]), spare
        for i in candidates:
            addition = min(most - counts[i], max(1, remaining * portions[i] // pool), spare)
            counts[i] = counts[i] + addition
            spare = spare - addition
    return np.array(counts)


def normal_values(stream_key, dims, spread, bound, pieces=(), kind=jnp.bfloat16):
    drawn = jax.random.normal(stream_key, dims, jnp.float32) * spread
    if len(pieces) > 0:
        drawn = block_levels(stream_key, dims, pieces, -0.22, 0.18) * drawn
    return jnp.clip(drawn, min=-bound, max=bound).astype(kind)


def setup_inputs(seed: int = 0) -> dict:
    seeds = jax.random.split(jax.random.key(seed), 7)
    tokens = normal_values(seeds[0], (TOKENS, D), 1.0, 6.0, ((0, 4), (1, 8)))
    expert_ids_keys = jax.random.split(jax.random.fold_in(seeds[1], 1), TOKENS // TOK_EP)
    expert_ids_turns = jax.random.permutation(jax.random.fold_in(seeds[1], 3), TOKENS // TOK_EP)
    expert_ids = jax.vmap(lambda own, number: shared_out(jax.random.fold_in(seeds[1], 2), own, number, TOK_EP, EXPERTS, TOP, CAP, 2))(expert_ids_keys, expert_ids_turns).reshape((TOKENS, TOP))
    combine_weights = jnp.clip(0.25 + 0.75 * jax.random.uniform(seeds[2], (TOKENS, TOP), jnp.float32) ** block_levels(seeds[2], (TOKENS, TOP), ((0, 4),), -0.2, 0.2), 0.25, 1.0)
    w_gate = normal_values(seeds[3], (EXPERTS, D, FF), D ** -0.5, 0.078125, ((0, 4), (2, 8)))
    w_up = normal_values(seeds[4], (EXPERTS, D, FF), D ** -0.5, 0.078125, ((0, 4), (2, 8)))
    w_down = normal_values(seeds[5], (EXPERTS, FF, D), FF ** -0.5, 0.0625, ((0, 4), (1, 8)))
    return dict(tokens=tokens, expert_ids=expert_ids, combine_weights=combine_weights, w_gate=w_gate, w_up=w_up, w_down=w_down)


def place_rows(buffer, where, values):
    return buffer.at[where].set(values)


def run_expert(operands):
    expert_rows, gate_w, up_w, down_w = operands
    gate_sums = jnp.dot(expert_rows, gate_w, preferred_element_type=jnp.float32)
    up_sums = jnp.dot(expert_rows, up_w, preferred_element_type=jnp.float32)
    hidden = (jax.nn.silu(gate_sums) * up_sums).astype(jnp.bfloat16)
    return jnp.dot(hidden, down_w, preferred_element_type=jnp.float32).astype(jnp.bfloat16)


def reference(tokens, expert_ids, combine_weights, w_gate, w_up, w_down):
    model_width = tokens.shape[1]
    blocks = tokens.reshape(N_EP, TOK_EP, model_width)
    chosen = expert_ids.reshape(N_EP, TOK_EP * TOP).astype(jnp.int32)
    expert_lane = jnp.arange(EXPERTS, dtype=jnp.int32)
    onehot = (chosen[:, :, None] == expert_lane[None, None, :]).astype(jnp.int32)
    before = jnp.cumsum(onehot, axis=1, dtype=jnp.int32) - onehot
    slot_index = jnp.sum(before * onehot, axis=2).astype(jnp.int32)
    position = (chosen * CAP + slot_index).astype(jnp.int32)
    source_rows = jnp.repeat(blocks, TOP, axis=1)
    dispatched = jnp.zeros((N_EP, EXPERTS * CAP, model_width), tokens.dtype)
    dispatched = jax.vmap(place_rows)(dispatched, position, source_rows)
    per_expert = dispatched.reshape(N_EP, EXPERTS, CAP, model_width).transpose(1, 0, 2, 3)
    per_expert = per_expert.reshape(EXPERTS, N_EP * CAP, model_width)
    expert_out = lax.map(run_expert, (per_expert, w_gate, w_up, w_down))
    expert_out = expert_out.reshape(EXPERTS, N_EP, CAP, model_width)
    group_index = jnp.arange(N_EP, dtype=jnp.int32)[:, None]
    picked = expert_out[chosen, group_index, slot_index].astype(jnp.float32)
    picked = picked.reshape(N_EP, TOK_EP, TOP, model_width)
    scales = combine_weights.reshape(N_EP, TOK_EP, TOP)[..., None]
    mixed_rows = jnp.sum(picked * scales, axis=2)
    return mixed_rows.reshape(TOKENS, model_width).astype(jnp.bfloat16)
```

```python
import jax
import jax.numpy as jnp
from jax import lax
from jax.experimental import pallas as pl
from jax.experimental.pallas import tpu as pltpu
from jax.sharding import PartitionSpec as P

MESH = pl.DeviceIdType.MESH
BF16 = jnp.bfloat16
F32 = jnp.float32


def kernel(
    tok, ids, wts, wg, wu, wd, out,
    rows_all, hid, wg_v, wu_v, wd_v, wt, wcol, acc,
    sib_r, s1s, s1r, s2s, s2r, s3s, s3r,
    load_sem, own_sem, ag_send_own, ag_send, ag_sib, ag_recv,
    wt_send, wt_recv, sib_ss, sib_rs, s1_ss, s1_rs, s2_ss, s2_rs, s3_ss, s3_rs,
):
    tok_rows, width = tok.shape
    half = tok_rows // 2
    ep = lax.axis_index("ep")
    fs = lax.axis_index("fsdp")
    y, x = ep // 2, ep % 2
    z, c = fs // 2, fs % 2
    group = [ep, ep + 1 - 2 * x, ep + 2 - 4 * y, 3 - ep]

    def sec(k, plane):
        core = c if plane == 0 else 1 - c
        return ((z + k) % 4) * 2 + core

    sib = (ep, z * 2 + 1 - c)
    x_nbr, y_nbr, diag = (group[1], fs), (group[2], fs), (group[3], fs)
    z_dev = [None] + [(ep, sec(k, 0)) for k in (1, 2, 3)]

    loads = [
        pltpu.make_async_copy(wg.at[0], wg_v, load_sem.at[0]),
        pltpu.make_async_copy(wu.at[0], wu_v, load_sem.at[1]),
        pltpu.make_async_copy(wd.at[0], wd_v, load_sem.at[2]),
    ]
    loads[0].start()
    loads[1].start()

    def grows(r, h):
        return pl.ds(pl.multiple_of(group[r] * tok_rows + h * half, half), half)

    def cols(s):
        return pl.ds(pl.multiple_of(s * width, 128), width)

    def block(r, h, k, plane):
        return rows_all.at[grows(r, h), cols(sec(k, plane))]

    own = pltpu.make_async_copy(
        tok,
        rows_all.at[pl.ds(pl.multiple_of(ep * tok_rows, tok_rows), tok_rows), cols(sec(0, 0))],
        own_sem,
    )
    own.start()

    lane_e = lax.broadcasted_iota(jnp.int32, (8, tok_rows), 0)
    wt[0] = jnp.where(ids[0:1, :] == lane_e, wts[0:1, :], 0.0) + jnp.where(
        ids[1:2, :] == lane_e, wts[1:2, :], 0.0
    )

    barrier = pltpu.get_barrier_semaphore()
    partners = [sib, x_nbr, y_nbr, diag, z_dev[1], z_dev[2], z_dev[3]]
    for dev in partners:
        pl.semaphore_signal(barrier, inc=1, device_id=dev, device_id_type=MESH)
    pl.semaphore_wait(barrier, len(partners))

    def rcopy(src, dst, ss, rs, dev):
        return pltpu.make_async_remote_copy(
            src_ref=src, dst_ref=dst, send_sem=ss, recv_sem=rs, device_id=dev, device_id_type=MESH
        )

    sent = []

    def send(src, dst, ss, rs, dev):
        d = rcopy(src, dst, ss, rs, dev)
        d.start()
        sent.append(d)

    def rsem(h, r, k, plane):
        return ag_recv.at[((h * 4 + r) * 4 + k) * 2 + plane]

    def src_of(r, h, k):
        if r == 0 and k == 0:
            return tok.at[pl.ds(h * half, half)]
        return block(r, h, k, 0)

    def to_x(r, h, k):
        send(src_of(r, h, k), block(r, h, k, 0), ag_send.at[(0 * 2 + h) * 16 + r * 4 + k], rsem(h, r ^ 1, k, 0), x_nbr)

    def to_y(r, h, k):
        send(src_of(r, h, k), block(r, h, k, 0), ag_send.at[(1 * 2 + h) * 16 + r * 4 + k], rsem(h, r ^ 2, k, 0), y_nbr)

    def to_sib(r, h, k):
        send(src_of(r, h, k), block(r, h, k, 0), ag_sib.at[h * 16 + r * 4 + k], rsem(h, r, k, 1), sib)

    def arrived(r, h, k, plane):
        b = block(r, h, k, plane)
        rcopy(b, b, ag_send.at[0], rsem(h, r, k, plane), sib).wait_recv()

    for h in (0, 1):
        to_x(0, h, 0)
        to_y(0, h, 0)
        for k in (1, 2, 3):
            send(
                src_of(0, h, 0), block(0, h, 0, 0), ag_send_own.at[h * 4 + k],
                rsem(h, 0, 4 - k, 0), z_dev[k],
            )
    for i, dev in ((1, x_nbr), (2, y_nbr), (3, diag)):
        send(wt.at[0], wt.at[i], wt_send.at[i], wt_recv.at[i], dev)
    for h in (0, 1):
        to_sib(0, h, 0)
    loads[2].start()

    def pass_on(k):
        arrived(1, 0, k, 0)
        to_y(1, 0, k)
        arrived(2, 1, k, 0)
        to_x(2, 1, k)
        to_sib(1, 0, k)
        to_sib(2, 1, k)

    for k in (1, 3, 2):
        for h in (0, 1):
            arrived(0, h, k, 0)
            to_x(0, h, k)
            to_y(0, h, k)
            to_sib(0, h, k)
        if k == 1:
            pass_on(0)
    for k in (1, 3, 2):
        pass_on(k)
    for k in (0, 1, 3, 2):
        for r, h in ((2, 0), (1, 1), (3, 0), (3, 1)):
            arrived(r, h, k, 0)
            to_sib(r, h, k)

    eye = lax.broadcasted_iota(jnp.int32, (tok_rows, tok_rows), 0) == lax.broadcasted_iota(
        jnp.int32, (tok_rows, tok_rows), 1
    )
    for r in range(4):
        if r > 0:
            rcopy(wt.at[r], wt.at[r], wt_send.at[0], wt_recv.at[r], sib).wait_recv()
        row = jnp.sum(jnp.where(lane_e == ep, wt[r], 0.0), axis=0, keepdims=True)
        col = jnp.sum(jnp.where(eye, row, 0.0), axis=1, keepdims=True)
        at = pl.ds(pl.multiple_of(group[r] * tok_rows, tok_rows), tok_rows)
        wcol[at, :] = jnp.broadcast_to(col, (tok_rows, 128))

    for r in range(4):
        for h in (0, 1):
            for k in range(4):
                arrived(r, h, k, 1)
    own.wait()
    for d in sent:
        d.wait_send()
    sent.clear()

    loads[0].wait()
    loads[1].wait()
    tile = 256

    @pl.loop(0, hid.shape[1] // tile)
    def _(i):
        at = pl.ds(pl.multiple_of(i * tile, tile), tile)
        g = jnp.dot(rows_all[...], wg_v[:, at], preferred_element_type=F32)
        u = jnp.dot(rows_all[...], wu_v[:, at], preferred_element_type=F32)
        hid[:, at] = (g / (1.0 + jnp.exp(-g)) * u).astype(BF16)

    loads[2].wait()

    def down(s, put):
        @pl.loop(0, width // tile)
        def _(i):
            off = pl.multiple_of(i * tile, tile)
            at = pl.ds(pl.multiple_of(s * width + i * tile, tile), tile)
            p = jnp.dot(hid[...], wd_v[:, at], preferred_element_type=F32)
            put(off, at, p * wcol[:, 0:1])

    steps = (1, 2, 3, 0)

    def stage0(j):
        k = steps[j]

        def put_sib(off, at, p):
            rows_all[:, at] = p.astype(BF16)

        def put_own(off, at, p):
            acc[j, :, pl.ds(off, tile)] = p

        down(sec(k, 1), put_sib)
        send(rows_all.at[:, cols(sec(k, 1))], sib_r.at[j], sib_ss.at[j], sib_rs.at[j], sib)
        down(sec(k, 0), put_own)

    def took(dst, rs):
        rcopy(dst, dst, ag_send.at[0], rs, sib).wait_recv()

    def stage1(j):
        took(sib_r.at[j], sib_rs.at[j])
        for h, gone, dev in ((0, (2, 3), y_nbr), (1, (1, 3), x_nbr)):
            for i, r in enumerate(gone):
                at = grows(r, h)
                s1s[j, h, i] = (acc[j, at, :] + sib_r[j, at, :].astype(F32)).astype(BF16)
            send(s1s.at[j, h], s1r.at[j, h], s1_ss.at[j * 2 + h], s1_rs.at[j * 2 + h], dev)
        for h, kept in ((0, (0, 1)), (1, (0, 2))):
            for r in kept:
                at = grows(r, h)
                acc[j, at, :] = acc[j, at, :] + sib_r[j, at, :].astype(F32)

    def stage2(j):
        for h, r, dev in ((0, 1, x_nbr), (1, 2, y_nbr)):
            took(s1r.at[j, h], s1_rs.at[j * 2 + h])
            s2s[j, h] = (acc[j, grows(r, h), :] + s1r[j, h, 1].astype(F32)).astype(BF16)
            send(s2s.at[j, h], s2r.at[j, h], s2_ss.at[j * 2 + h], s2_rs.at[j * 2 + h], dev)

    def stage3(j):
        k = steps[j]
        for h in (0, 1):
            took(s2r.at[j, h], s2_rs.at[j * 2 + h])
            v = acc[j, grows(0, h), :] + s1r[j, h, 0].astype(F32) + s2r[j, h].astype(F32)
            if k != 0:
                s3s[j, h] = v.astype(BF16)
                send(s3s.at[j, h], s3r.at[j, h], s3_ss.at[j * 2 + h], s3_rs.at[j * 2 + h], z_dev[k])
            else:
                for i in range(3):
                    took(s3r.at[i, h], s3_rs.at[i * 2 + h])
                    v = v + s3r[i, h].astype(F32)
                out[pl.ds(h * half, half), :] = v.astype(BF16)

    stage0(0)
    stage1(0)
    stage0(1)
    stage1(1)
    stage2(0)
    stage0(2)
    stage1(2)
    stage2(1)
    stage0(3)
    stage1(3)
    stage3(0)
    stage2(2)
    stage3(1)
    stage2(3)
    stage3(2)
    stage3(3)
    for d in sent:
        d.wait_send()


def fused(tokens, expert_ids, combine_weights, w_gate, w_up, w_down):
    tok_rows, width = tokens.shape
    model = w_gate.shape[1]
    hidden = w_gate.shape[2]
    total = 4 * tok_rows
    half = tok_rows // 2
    vm = pl.BlockSpec(memory_space=pltpu.VMEM)
    hbm = pl.BlockSpec(memory_space=pl.ANY)
    dma = lambda n: pltpu.SemaphoreType.DMA((n,))
    return pl.pallas_call(
        kernel,
        out_shape=jax.ShapeDtypeStruct((tok_rows, width), BF16),
        in_specs=[vm, vm, vm, hbm, hbm, hbm],
        out_specs=vm,
        scratch_shapes=[
            pltpu.VMEM((total, model), BF16),
            pltpu.VMEM((total, hidden), BF16),
            pltpu.VMEM((model, hidden), BF16),
            pltpu.VMEM((model, hidden), BF16),
            pltpu.VMEM((hidden, model), BF16),
            pltpu.VMEM((4, 8, tok_rows), F32),
            pltpu.VMEM((total, 128), F32),
            pltpu.VMEM((4, total, width), F32),
            pltpu.VMEM((4, total, width), BF16),
            pltpu.VMEM((4, 2, 2, half, width), BF16),
            pltpu.VMEM((4, 2, 2, half, width), BF16),
            pltpu.VMEM((4, 2, half, width), BF16),
            pltpu.VMEM((4, 2, half, width), BF16),
            pltpu.VMEM((3, 2, half, width), BF16),
            pltpu.VMEM((3, 2, half, width), BF16),
            dma(3),
            pltpu.SemaphoreType.DMA,
            dma(8), dma(64), dma(32), dma(64),
            dma(4), dma(4), dma(4), dma(4), dma(8), dma(8), dma(8), dma(8), dma(6), dma(6),
        ],
        compiler_params=pltpu.CompilerParams(
            collective_id=0, has_side_effects=True, vmem_limit_bytes=63 * 1024 * 1024
        ),
        cost_estimate=pl.CostEstimate(
            flops=6 * total * model * hidden,
            bytes_accessed=6 * model * hidden,
            transcendentals=total * hidden,
        ),
    )(tokens, expert_ids.T, combine_weights.T, w_gate, w_up, w_down)


def shards(tokens, expert_ids, combine_weights, w_gate, w_up, w_down):
    groups = lax.axis_size("ep")
    tok_rows = tokens.shape[0]
    width_local = tokens.shape[1]
    capacity = min(tok_rows, 4 * tok_rows // groups)
    experts_all = groups * w_gate.shape[0]
    chosen = expert_ids.reshape(-1)
    expert_lane = jnp.arange(experts_all, dtype=jnp.int32)
    onehot = (chosen[:, None] == expert_lane[None, :]).astype(jnp.int32)
    before = jnp.cumsum(onehot, axis=0, dtype=jnp.int32) - onehot
    slot_index = jnp.sum(before * onehot, axis=1)
    position = (chosen * capacity + slot_index).reshape(tok_rows, 2)
    places = jnp.arange(experts_all * capacity, dtype=jnp.int32)
    select = position[:, :, None] == places[None, None, :]
    dispatch = jnp.sum(select.astype(jnp.float32), axis=1).astype(jnp.bfloat16)
    packed = lax.dot_general(
        dispatch, tokens, (((0,), (0,)), ((), ())), preferred_element_type=jnp.float32
    )
    packed = packed.astype(jnp.bfloat16).reshape(experts_all, capacity, width_local)
    arrived = lax.all_to_all(packed, "ep", split_axis=0, concat_axis=0, tiled=True)
    expert_rows = arrived.reshape(groups * capacity, width_local)
    gate_local = w_gate[0]
    up_local = w_up[0]
    down_local = w_down[0]
    section = lax.all_gather(expert_rows, "fsdp", axis=1, tiled=True)
    gate_sums = jnp.dot(section, gate_local, preferred_element_type=jnp.float32)
    up_sums = jnp.dot(section, up_local, preferred_element_type=jnp.float32)
    hidden = (jax.nn.silu(gate_sums) * up_sums).astype(jnp.bfloat16)
    summed = lax.psum_scatter(
        lax.dot_general(
            down_local, hidden, (((0,), (1,)), ((), ())), preferred_element_type=jnp.float32
        ),
        "fsdp",
        scatter_dimension=0,
        tiled=True,
    )
    result = summed.T.astype(jnp.bfloat16)
    returned = lax.all_to_all(
        result.reshape(groups, capacity, width_local), "ep", split_axis=0, concat_axis=0, tiled=True
    )
    weighting = jnp.sum(jnp.where(select, combine_weights[:, :, None], 0.0), axis=1)
    mixed_rows = jnp.dot(
        weighting,
        returned.reshape(-1, width_local).astype(jnp.float32),
        precision=lax.Precision.HIGHEST,
    )
    return mixed_rows.astype(jnp.bfloat16)


def solution(mesh):
    in_specs = (
        P("ep", "fsdp"),
        P("ep", None),
        P("ep", None),
        P("ep", None, "fsdp"),
        P("ep", None, "fsdp"),
        P("ep", "fsdp", None),
    )
    out_specs = P("ep", "fsdp")

    def layer(tokens, *rest):
        small = mesh.shape["ep"] == 4 and mesh.shape["fsdp"] == 8
        return (fused if small else shards)(tokens, *rest)

    return jax.shard_map(layer, mesh=mesh, in_specs=in_specs, out_specs=out_specs, check_vma=False)
```

```python
import jax
import jax.numpy as jnp
from jax import lax
from jax.experimental import pallas as pl
from jax.experimental.pallas import tpu as pltpu
from jax.sharding import PartitionSpec as P

MESH = pl.DeviceIdType.MESH
BF16 = jnp.bfloat16
F32 = jnp.float32


def kernel(
    tok, ids, wts, wg, wu, wd, out,
    rows_all, hid, wg_v, wu_v, wd_v, wt, wcol, acc,
    sib_r, s1s, s1r, s2s, s2r, s3s, s3r,
    load_sem, own_sem, ag_send_own, ag_send, ag_sib, ag_recv,
    wt_send, wt_recv, sib_ss, sib_rs, s1_ss, s1_rs, s2_ss, s2_rs, s3_ss, s3_rs,
):
    tok_rows, width = tok.shape
    part = tok_rows // 2
    half = tok_rows // 4
    ep = lax.axis_index("ep")
    fs = lax.axis_index("fsdp")
    y, x = ep // 2, ep % 2
    z, c = fs // 2, fs % 2
    group = [ep, ep + 1 - 2 * x, ep + 2 - 4 * y, 3 - ep]

    def sec(k, plane):
        core = c if plane == 0 else 1 - c
        return ((z + k) % 4) * 2 + core

    sib = (ep, z * 2 + 1 - c)
    x_nbr, y_nbr, diag = (group[1], fs), (group[2], fs), (group[3], fs)
    z_dev = [None] + [(ep, sec(k, 0)) for k in (1, 2, 3)]

    loads = [
        pltpu.make_async_copy(wg.at[0], wg_v, load_sem.at[0]),
        pltpu.make_async_copy(wu.at[0], wu_v, load_sem.at[1]),
        pltpu.make_async_copy(wd.at[0], wd_v, load_sem.at[2]),
    ]
    loads[0].start()
    loads[1].start()

    def grows(r, h):
        return pl.ds(pl.multiple_of(group[r] * part + h * half, half), half)

    def cols(s):
        return pl.ds(pl.multiple_of(s * width, 128), width)

    def block(b, r, h, k, plane):
        return rows_all.at[b, grows(r, h), cols(sec(k, plane))]

    own = [
        pltpu.make_async_copy(
            tok.at[pl.ds(b * part, part)],
            rows_all.at[b, pl.ds(pl.multiple_of(ep * part, part), part), cols(sec(0, 0))],
            own_sem.at[b],
        )
        for b in (0, 1)
    ]
    own[0].start()
    own[1].start()

    lane_e = lax.broadcasted_iota(jnp.int32, (8, tok_rows), 0)
    wt[0] = jnp.where(ids[0:1, :] == lane_e, wts[0:1, :], 0.0) + jnp.where(
        ids[1:2, :] == lane_e, wts[1:2, :], 0.0
    )

    barrier = pltpu.get_barrier_semaphore()
    partners = [sib, x_nbr, y_nbr, diag, z_dev[1], z_dev[2], z_dev[3]]
    for dev in partners:
        pl.semaphore_signal(barrier, inc=1, device_id=dev, device_id_type=MESH)
    pl.semaphore_wait(barrier, len(partners))

    def rcopy(src, dst, ss, rs, dev):
        return pltpu.make_async_remote_copy(
            src_ref=src, dst_ref=dst, send_sem=ss, recv_sem=rs, device_id=dev, device_id_type=MESH
        )

    sent = {0: [], 1: [], 2: []}

    def send(lot, src, dst, ss, rs, dev):
        d = rcopy(src, dst, ss, rs, dev)
        d.start()
        sent[lot].append(d)

    def rsem(b, h, r, k, plane):
        return ag_recv.at[(((b * 2 + h) * 4 + r) * 4 + k) * 2 + plane]

    def src_of(b, r, h, k):
        if r == 0 and k == 0:
            return tok.at[pl.ds(b * part + h * half, half)]
        return block(b, r, h, k, 0)

    def to_x(b, r, h, k):
        send(b, src_of(b, r, h, k), block(b, r, h, k, 0),
             ag_send.at[(b * 2 + h) * 16 + r * 4 + k], rsem(b, h, r ^ 1, k, 0), x_nbr)

    def to_y(b, r, h, k):
        send(b, src_of(b, r, h, k), block(b, r, h, k, 0),
             ag_send.at[64 + (b * 2 + h) * 16 + r * 4 + k], rsem(b, h, r ^ 2, k, 0), y_nbr)

    def to_sib(b, r, h, k):
        send(b, src_of(b, r, h, k), block(b, r, h, k, 0),
             ag_sib.at[(b * 2 + h) * 16 + r * 4 + k], rsem(b, h, r, k, 1), sib)

    def arrived(b, r, h, k, plane):
        at = block(b, r, h, k, plane)
        rcopy(at, at, ag_send.at[0], rsem(b, h, r, k, plane), sib).wait_recv()

    def own_z(b):
        for h in (0, 1):
            for k in (1, 2, 3):
                send(b, src_of(b, 0, h, 0), block(b, 0, h, 0, 0),
                     ag_send_own.at[(b * 2 + h) * 4 + k], rsem(b, h, 0, 4 - k, 0), z_dev[k])

    def own_xy(b):
        for h in (0, 1):
            to_x(b, 0, h, 0)
            to_y(b, 0, h, 0)

    def own_sib(b):
        for h in (0, 1):
            to_sib(b, 0, h, 0)

    def from_z(b, k):
        for h in (0, 1):
            arrived(b, 0, h, k, 0)
            to_x(b, 0, h, k)
            to_y(b, 0, h, k)
            to_sib(b, 0, h, k)

    def pass_on(b, k):
        arrived(b, 1, 0, k, 0)
        to_y(b, 1, 0, k)
        arrived(b, 2, 1, k, 0)
        to_x(b, 2, 1, k)
        to_sib(b, 1, 0, k)
        to_sib(b, 2, 1, k)

    def last(b, k):
        for r, h in ((2, 0), (1, 1), (3, 0), (3, 1)):
            arrived(b, r, h, k, 0)
            to_sib(b, r, h, k)

    def gathered(b):
        for r in range(4):
            for h in (0, 1):
                for k in range(4):
                    arrived(b, r, h, k, 1)
        own[b].wait()

    def all_sent(lot):
        for d in sent[lot]:
            d.wait_send()
        sent[lot].clear()

    own_z(0)
    own_xy(0)
    for i, dev in ((1, x_nbr), (2, y_nbr), (3, diag)):
        send(2, wt.at[0], wt.at[i], wt_send.at[i], wt_recv.at[i], dev)
    own_sib(0)
    own_xy(1)
    own_sib(1)
    loads[2].start()
    from_z(0, 1)
    pass_on(0, 0)
    from_z(0, 3)
    from_z(0, 2)
    own_z(1)
    for k in (1, 3, 2):
        pass_on(0, k)
    for k in (0, 1, 3, 2):
        last(0, k)

    eye = lax.broadcasted_iota(jnp.int32, (tok_rows, tok_rows), 0) == lax.broadcasted_iota(
        jnp.int32, (tok_rows, tok_rows), 1
    )
    for r in range(4):
        if r > 0:
            rcopy(wt.at[r], wt.at[r], wt_send.at[0], wt_recv.at[r], sib).wait_recv()
        row = jnp.sum(jnp.where(lane_e == ep, wt[r], 0.0), axis=0, keepdims=True)
        col = jnp.sum(jnp.where(eye, row, 0.0), axis=1, keepdims=True)
        at = pl.ds(pl.multiple_of(group[r] * part, part), part)
        for b in (0, 1):
            wcol[b, at, :] = jnp.broadcast_to(col[b * part:(b + 1) * part], (part, 128))

    tile = hid.shape[2] // 4

    def up(b, i):
        at = pl.ds(i * tile, tile)
        g = jnp.dot(rows_all[b], wg_v[:, at], preferred_element_type=F32)
        u = jnp.dot(rows_all[b], wu_v[:, at], preferred_element_type=F32)
        hid[b, :, at] = (g / (1.0 + jnp.exp(-g)) * u).astype(BF16)

    steps = (1, 2, 3, 0)

    def down(b, s):
        p = jnp.dot(hid[b], wd_v[:, cols(s)], preferred_element_type=F32)
        return p * wcol[b, :, 0:1]

    def stage0(b, j):
        k = steps[j]
        s = cols(sec(k, 1))
        rows_all[b, :, s] = down(b, sec(k, 1)).astype(BF16)
        send(2, rows_all.at[b, :, s], sib_r.at[b, j], sib_ss.at[b * 4 + j], sib_rs.at[b * 4 + j], sib)
        acc[b, j] = down(b, sec(k, 0))

    def took(dst, rs):
        rcopy(dst, dst, ag_send.at[0], rs, sib).wait_recv()

    def stage1(b, j):
        took(sib_r.at[b, j], sib_rs.at[b * 4 + j])
        for h, gone, dev in ((0, (2, 3), y_nbr), (1, (1, 3), x_nbr)):
            n = (b * 4 + j) * 2 + h
            for i, r in enumerate(gone):
                at = grows(r, h)
                s1s[b, j, h, i] = (acc[b, j, at, :] + sib_r[b, j, at, :].astype(F32)).astype(BF16)
            send(2, s1s.at[b, j, h], s1r.at[b, j, h], s1_ss.at[n], s1_rs.at[n], dev)
        for h, kept in ((0, (0, 1)), (1, (0, 2))):
            for r in kept:
                at = grows(r, h)
                acc[b, j, at, :] = acc[b, j, at, :] + sib_r[b, j, at, :].astype(F32)

    def stage2(b, j):
        for h, r, dev in ((0, 1, x_nbr), (1, 2, y_nbr)):
            n = (b * 4 + j) * 2 + h
            took(s1r.at[b, j, h], s1_rs.at[n])
            s2s[b, j, h] = (acc[b, j, grows(r, h), :] + s1r[b, j, h, 1].astype(F32)).astype(BF16)
            send(2, s2s.at[b, j, h], s2r.at[b, j, h], s2_ss.at[n], s2_rs.at[n], dev)

    def stage3(b, j):
        k = steps[j]
        for h in (0, 1):
            n = (b * 4 + j) * 2 + h
            took(s2r.at[b, j, h], s2_rs.at[n])
            v = acc[b, j, grows(0, h), :] + s1r[b, j, h, 0].astype(F32) + s2r[b, j, h].astype(F32)
            if k != 0:
                n = (b * 3 + j) * 2 + h
                s3s[b, j, h] = v.astype(BF16)
                send(2, s3s.at[b, j, h], s3r.at[b, j, h], s3_ss.at[n], s3_rs.at[n], z_dev[k])
            else:
                for i in range(3):
                    took(s3r.at[b, i, h], s3_rs.at[(b * 3 + i) * 2 + h])
                    v = v + s3r[b, i, h].astype(F32)
                out[pl.ds(b * part + h * half, half), :] = v.astype(BF16)

    for k in (1, 3, 2):
        from_z(1, k)
    gathered(0)
    loads[0].wait()
    loads[1].wait()
    up(0, 0)
    pass_on(1, 0)
    pass_on(1, 1)
    up(0, 1)
    pass_on(1, 3)
    pass_on(1, 2)
    up(0, 2)
    last(1, 0)
    up(0, 3)
    last(1, 1)
    all_sent(0)
    loads[2].wait()
    stage0(0, 0)
    last(1, 3)
    stage0(0, 1)
    stage1(0, 0)
    last(1, 2)
    stage0(0, 2)
    stage1(0, 1)
    stage0(0, 3)
    stage1(0, 2)
    stage1(0, 3)
    gathered(1)
    up(1, 0)
    stage2(0, 0)
    stage2(0, 1)
    up(1, 1)
    stage2(0, 2)
    stage3(0, 0)
    up(1, 2)
    stage2(0, 3)
    stage3(0, 1)
    up(1, 3)
    stage3(0, 2)
    all_sent(1)
    stage0(1, 0)
    stage0(1, 1)
    stage1(1, 0)
    stage0(1, 2)
    stage1(1, 1)
    stage0(1, 3)
    stage1(1, 2)
    stage2(1, 0)
    stage1(1, 3)
    stage3(0, 3)
    stage2(1, 1)
    stage3(1, 0)
    stage2(1, 2)
    stage3(1, 1)
    stage2(1, 3)
    stage3(1, 2)
    stage3(1, 3)
    all_sent(2)


def fused(tokens, expert_ids, combine_weights, w_gate, w_up, w_down):
    tok_rows, width = tokens.shape
    model = w_gate.shape[1]
    hidden = w_gate.shape[2]
    total = 2 * tok_rows
    half = tok_rows // 4
    vm = pl.BlockSpec(memory_space=pltpu.VMEM)
    hbm = pl.BlockSpec(memory_space=pl.ANY)
    dma = lambda n: pltpu.SemaphoreType.DMA((n,))
    return pl.pallas_call(
        kernel,
        out_shape=jax.ShapeDtypeStruct((tok_rows, width), BF16),
        in_specs=[vm, vm, vm, hbm, hbm, hbm],
        out_specs=vm,
        scratch_shapes=[
            pltpu.VMEM((2, total, model), BF16),
            pltpu.VMEM((2, total, hidden), BF16),
            pltpu.VMEM((model, hidden), BF16),
            pltpu.VMEM((model, hidden), BF16),
            pltpu.VMEM((hidden, model), BF16),
            pltpu.VMEM((4, 8, tok_rows), F32),
            pltpu.VMEM((2, total, 128), F32),
            pltpu.VMEM((2, 4, total, width), F32),
            pltpu.VMEM((2, 4, total, width), BF16),
            pltpu.VMEM((2, 4, 2, 2, half, width), BF16),
            pltpu.VMEM((2, 4, 2, 2, half, width), BF16),
            pltpu.VMEM((2, 4, 2, half, width), BF16),
            pltpu.VMEM((2, 4, 2, half, width), BF16),
            pltpu.VMEM((2, 3, 2, half, width), BF16),
            pltpu.VMEM((2, 3, 2, half, width), BF16),
            dma(3),
            dma(2),
            dma(16), dma(128), dma(64), dma(128),
            dma(4), dma(4), dma(8), dma(8), dma(16), dma(16), dma(16), dma(16), dma(12), dma(12),
        ],
        compiler_params=pltpu.CompilerParams(
            collective_id=0, has_side_effects=True, vmem_limit_bytes=63 * 1024 * 1024
        ),
        cost_estimate=pl.CostEstimate(
            flops=12 * total * model * hidden,
            bytes_accessed=6 * model * hidden,
            transcendentals=2 * total * hidden,
        ),
    )(tokens, expert_ids.T, combine_weights.T, w_gate, w_up, w_down)


def shards(tokens, expert_ids, combine_weights, w_gate, w_up, w_down):
    groups = lax.axis_size("ep")
    tok_rows = tokens.shape[0]
    width_local = tokens.shape[1]
    capacity = min(tok_rows, 4 * tok_rows // groups)
    experts_all = groups * w_gate.shape[0]
    chosen = expert_ids.reshape(-1)
    expert_lane = jnp.arange(experts_all, dtype=jnp.int32)
    onehot = (chosen[:, None] == expert_lane[None, :]).astype(jnp.int32)
    before = jnp.cumsum(onehot, axis=0, dtype=jnp.int32) - onehot
    slot_index = jnp.sum(before * onehot, axis=1)
    position = (chosen * capacity + slot_index).reshape(tok_rows, 2)
    places = jnp.arange(experts_all * capacity, dtype=jnp.int32)
    select = position[:, :, None] == places[None, None, :]
    dispatch = jnp.sum(select.astype(jnp.float32), axis=1).astype(jnp.bfloat16)
    packed = lax.dot_general(
        dispatch, tokens, (((0,), (0,)), ((), ())), preferred_element_type=jnp.float32
    )
    packed = packed.astype(jnp.bfloat16).reshape(experts_all, capacity, width_local)
    arrived = lax.all_to_all(packed, "ep", split_axis=0, concat_axis=0, tiled=True)
    expert_rows = arrived.reshape(groups * capacity, width_local)
    gate_local = w_gate[0]
    up_local = w_up[0]
    down_local = w_down[0]
    section = lax.all_gather(expert_rows, "fsdp", axis=1, tiled=True)
    gate_sums = jnp.dot(section, gate_local, preferred_element_type=jnp.float32)
    up_sums = jnp.dot(section, up_local, preferred_element_type=jnp.float32)
    hidden = (jax.nn.silu(gate_sums) * up_sums).astype(jnp.bfloat16)
    summed = lax.psum_scatter(
        lax.dot_general(
            down_local, hidden, (((0,), (1,)), ((), ())), preferred_element_type=jnp.float32
        ),
        "fsdp",
        scatter_dimension=0,
        tiled=True,
    )
    result = summed.T.astype(jnp.bfloat16)
    returned = lax.all_to_all(
        result.reshape(groups, capacity, width_local), "ep", split_axis=0, concat_axis=0, tiled=True
    )
    weighting = jnp.sum(jnp.where(select, combine_weights[:, :, None], 0.0), axis=1)
    mixed_rows = jnp.dot(
        weighting,
        returned.reshape(-1, width_local).astype(jnp.float32),
        precision=lax.Precision.HIGHEST,
    )
    return mixed_rows.astype(jnp.bfloat16)


def solution(mesh):
    in_specs = (
        P("ep", "fsdp"),
        P("ep", None),
        P("ep", None),
        P("ep", None, "fsdp"),
        P("ep", None, "fsdp"),
        P("ep", "fsdp", None),
    )
    out_specs = P("ep", "fsdp")

    def layer(tokens, *rest):
        small = mesh.shape["ep"] == 4 and mesh.shape["fsdp"] == 8
        return (fused if small else shards)(tokens, *rest)

    return jax.shard_map(layer, mesh=mesh, in_specs=in_specs, out_specs=out_specs, check_vma=False)
```

```python
import jax
import jax.numpy as jnp
from jax import lax
from jax.experimental import pallas as pl
from jax.experimental.pallas import tpu as pltpu
from jax.sharding import PartitionSpec as P

MESH = pl.DeviceIdType.MESH
BF16 = jnp.bfloat16
F32 = jnp.float32


def kernel(
    tok, ids, wts, wg, wu, wd, out,
    rows_all, hid, wg_v, wu_v, wd_v, wt, wcol, acc,
    sib_r, s1s, s1r, s2s, s2r, s3s, s3r,
    load_sem, own_sem, z_ss, z_rs, h1_ss, h1_rs, h2_ss, h2_rs, c0_ss, c0_rs, c1_ss, c1_rs,
    wt_send, wt_recv, sib_ss, sib_rs, s1_ss, s1_rs, s2_ss, s2_rs, s3_ss, s3_rs,
):
    tok_rows, width = tok.shape
    part = tok_rows // 2
    half = tok_rows // 4
    ep = lax.axis_index("ep")
    fs = lax.axis_index("fsdp")
    y, x = ep // 2, ep % 2
    z, c = fs // 2, fs % 2
    group = [ep, ep + 1 - 2 * x, ep + 2 - 4 * y, 3 - ep]

    def sec(k, plane):
        core = c if plane == 0 else 1 - c
        return ((z + k) % 4) * 2 + core

    sib = (ep, z * 2 + 1 - c)
    x_nbr, y_nbr, diag = (group[1], fs), (group[2], fs), (group[3], fs)
    z_dev = [None] + [(ep, sec(k, 0)) for k in (1, 2, 3)]

    loads = [
        pltpu.make_async_copy(wg.at[0], wg_v, load_sem.at[0]),
        pltpu.make_async_copy(wu.at[0], wu_v, load_sem.at[1]),
        pltpu.make_async_copy(wd.at[0], wd_v, load_sem.at[2]),
    ]

    def place(r, h):
        gy = y if r < 2 else 1 - y
        gx = x if r % 2 == 0 else 1 - x
        return gy * 2 + gx if h == 0 else gx * 2 + gy

    def grows(r, h):
        return pl.ds(pl.multiple_of(h * part * 2 + place(r, h) * half, half), half)

    def prows(h, other):
        first = y if h == 0 else x
        if other:
            first = 1 - first
        return pl.ds(pl.multiple_of(h * part * 2 + first * part, part), part)

    def cols(s):
        return pl.ds(pl.multiple_of(s * width, 128), width)

    def own_block(b, h, k):
        return rows_all.at[b, grows(0, h), cols(sec(k, 0))]

    def pair(b, h, k, other, plane=0):
        return rows_all.at[b, prows(h, other), cols(sec(k, plane))]

    def tok_part(b, h):
        return tok.at[pl.ds(b * part + h * half, half)]

    both = [(b, h) for b in (0, 1) for h in (0, 1)]
    own = [
        pltpu.make_async_copy(tok_part(b, h), own_block(b, h, 0), own_sem.at[b * 2 + h])
        for b, h in both
    ]
    for d in own:
        d.start()

    lane_e = lax.broadcasted_iota(jnp.int32, (8, tok_rows), 0)
    wt[0] = jnp.where(ids[0:1, :] == lane_e, wts[0:1, :], 0.0) + jnp.where(
        ids[1:2, :] == lane_e, wts[1:2, :], 0.0
    )

    barrier = pltpu.get_barrier_semaphore()
    partners = [sib, x_nbr, y_nbr, diag, z_dev[1], z_dev[2], z_dev[3]]
    for dev in partners:
        pl.semaphore_signal(barrier, inc=1, device_id=dev, device_id_type=MESH)
    loads[0].start()
    loads[1].start()
    for d in own:
        d.wait()
    pl.semaphore_wait(barrier, len(partners))

    def rcopy(src, dst, ss, rs, dev):
        return pltpu.make_async_remote_copy(
            src_ref=src, dst_ref=dst, send_sem=ss, recv_sem=rs, device_id=dev, device_id_type=MESH
        )

    def send(src, dst, ss, rs, dev):
        rcopy(src, dst, ss, rs, dev).start()

    def took(dst, rs):
        rcopy(dst, dst, z_ss.at[0], rs, sib).wait_recv()

    def left(src, ss):
        rcopy(src, src, ss, z_rs.at[0], sib).wait_send()

    def num(b, h, k):
        return (b * 2 + h) * 4 + k

    def own_z(b):
        for h in (0, 1):
            for k in (1, 2, 3):
                send(tok_part(b, h), own_block(b, h, 0), z_ss.at[num(b, h, k)],
                     z_rs.at[num(b, h, 4 - k)], z_dev[k])

    def first(b, k):
        for h, dev in ((0, x_nbr), (1, y_nbr)):
            n = num(b, h, k)
            at = own_block(b, h, k)
            if k != 0:
                took(at, z_rs.at[n])
            send(at, at, h1_ss.at[n], h1_rs.at[n], dev)

    def second(b, k):
        for h, r, dev in ((0, 1, y_nbr), (1, 2, x_nbr)):
            n = num(b, h, k)
            took(rows_all.at[b, grows(r, h), cols(sec(k, 0))], h1_rs.at[n])
            at = pair(b, h, k, False)
            send(at, at, h2_ss.at[n], h2_rs.at[n], dev)
            send(at, at, c0_ss.at[n], c0_rs.at[n], sib)

    def last(b, k):
        for h in (0, 1):
            n = num(b, h, k)
            at = pair(b, h, k, True)
            took(at, h2_rs.at[n])
            send(at, at, c1_ss.at[n], c1_rs.at[n], sib)

    def gathered(b):
        @pl.loop(0, 4)
        def _(k):
            for h in (0, 1):
                took(pair(b, h, k, False, 1), c0_rs.at[num(b, h, k)])
                took(pair(b, h, k, True, 1), c1_rs.at[num(b, h, k)])

    def all_sent(b):
        @pl.loop(0, 4)
        def _(k):
            for h in (0, 1):
                n = num(b, h, k)
                left(own_block(b, h, k), h1_ss.at[n])
                left(pair(b, h, k, False), h2_ss.at[n])
                left(pair(b, h, k, False), c0_ss.at[n])
                left(pair(b, h, k, True), c1_ss.at[n])

        for h in (0, 1):
            for k in (1, 2, 3):
                left(tok_part(b, h), z_ss.at[num(b, h, k)])

    own_z(0)
    first(0, 0)
    for i, dev in ((1, x_nbr), (2, y_nbr), (3, diag)):
        send(wt.at[0], wt.at[i], wt_send.at[i], wt_recv.at[i], dev)
    loads[2].start()
    second(0, 0)
    first(0, 1)
    first(0, 3)
    first(0, 2)
    own_z(1)
    first(1, 0)
    second(0, 1)
    second(0, 3)
    second(0, 2)

    eye = lax.broadcasted_iota(jnp.int32, (tok_rows, tok_rows), 0) == lax.broadcasted_iota(
        jnp.int32, (tok_rows, tok_rows), 1
    )
    for r in range(4):
        if r > 0:
            took(wt.at[r], wt_recv.at[r])
        row = jnp.sum(jnp.where(lane_e == ep, wt[r], 0.0), axis=0, keepdims=True)
        col = jnp.sum(jnp.where(eye, row, 0.0), axis=1, keepdims=True)
        for b, h in both:
            lo = b * part + h * half
            wcol[b, grows(r, h), :] = jnp.broadcast_to(col[lo:lo + half], (half, 128))

    for k in (0, 1, 3, 2):
        last(0, k)
    for k in (1, 3, 2):
        first(1, k)

    tile = hid.shape[2] // 4

    def up(b, i):
        at = pl.ds(pl.multiple_of(i * tile, tile), tile)
        g = jnp.dot(rows_all[b], wg_v[:, at], preferred_element_type=F32)
        u = jnp.dot(rows_all[b], wu_v[:, at], preferred_element_type=F32)
        hid[b, :, at] = (g / (1.0 + jnp.exp(-g)) * u).astype(BF16)

    def down(b, s):
        p = jnp.dot(hid[b], wd_v[:, cols(s)], preferred_element_type=F32)
        return p * wcol[b, :, 0:1]

    def stage0(b, j):
        k = (j + 1) % 4
        s = cols(sec(k, 1))
        n = b * 4 + j
        rows_all[b, :, s] = down(b, sec(k, 1)).astype(BF16)
        send(rows_all.at[b, :, s], sib_r.at[b, j], sib_ss.at[n], sib_rs.at[n], sib)
        acc[b, j] = down(b, sec(k, 0))

    def stage1(b, j):
        took(sib_r.at[b, j], sib_rs.at[b * 4 + j])
        for h, gone, dev in ((0, (2, 3), y_nbr), (1, (1, 3), x_nbr)):
            n = (b * 4 + j) * 2 + h
            for i, r in enumerate(gone):
                at = grows(r, h)
                s1s[b, j, h, i] = (acc[b, j, at, :] + sib_r[b, j, at, :].astype(F32)).astype(BF16)
            send(s1s.at[b, j, h], s1r.at[b, j, h], s1_ss.at[n], s1_rs.at[n], dev)
        for h, kept in ((0, (0, 1)), (1, (0, 2))):
            for r in kept:
                at = grows(r, h)
                acc[b, j, at, :] = acc[b, j, at, :] + sib_r[b, j, at, :].astype(F32)

    def stage2(b, j):
        for h, r, dev in ((0, 1, x_nbr), (1, 2, y_nbr)):
            n = (b * 4 + j) * 2 + h
            took(s1r.at[b, j, h], s1_rs.at[n])
            s2s[b, j, h] = (acc[b, j, grows(r, h), :] + s1r[b, j, h, 1].astype(F32)).astype(BF16)
            send(s2s.at[b, j, h], s2r.at[b, j, h], s2_ss.at[n], s2_rs.at[n], dev)

    def summed(b, j, h):
        took(s2r.at[b, j, h], s2_rs.at[(b * 4 + j) * 2 + h])
        return acc[b, j, grows(0, h), :] + s1r[b, j, h, 0].astype(F32) + s2r[b, j, h].astype(F32)

    def stage3(b, j):
        for h in (0, 1):
            n = (b * 3 + j) * 2 + h
            s3s[b, j, h] = summed(b, j, h).astype(BF16)
            send(s3s.at[b, j, h], s3r.at[b, j, h], s3_ss.at[n], s3_rs.at[n], (ep, sec(j + 1, 0)))

    def finish(b):
        for h in (0, 1):
            v = summed(b, 3, h)
            for i in range(3):
                took(s3r.at[b, i, h], s3_rs.at[(b * 3 + i) * 2 + h])
                v = v + s3r[b, i, h].astype(F32)
            out[pl.ds(b * part + h * half, half), :] = v.astype(BF16)

    gathered(0)
    loads[0].wait()
    loads[1].wait()

    @pl.loop(0, 4)
    def _(i):
        up(0, i)
        second(1, i)

    all_sent(0)
    loads[2].wait()

    @pl.loop(0, 4)
    def _(j):
        stage0(0, j)
        last(1, j)

        @pl.when(j > 0)
        def _():
            stage1(0, j - 1)

    stage1(0, 3)
    gathered(1)

    @pl.loop(0, 4)
    def _(i):
        up(1, i)
        stage2(0, i)

        @pl.when(i > 0)
        def _():
            stage3(0, i - 1)

    all_sent(1)

    @pl.loop(0, 4)
    def _(j):
        stage0(1, j)

        @pl.when(j > 0)
        def _():
            stage1(1, j - 1)

        @pl.when(j > 1)
        def _():
            stage2(1, j - 2)

    stage1(1, 3)
    stage2(1, 2)
    stage3(1, 0)
    finish(0)
    stage3(1, 1)
    stage2(1, 3)
    stage3(1, 2)
    finish(1)

    for i in (1, 2, 3):
        left(wt.at[0], wt_send.at[i])
    for b in (0, 1):
        @pl.loop(0, 4)
        def _(j):
            left(sib_r.at[b, j], sib_ss.at[b * 4 + j])
            for h in (0, 1):
                left(s1s.at[b, j, h], s1_ss.at[(b * 4 + j) * 2 + h])
                left(s2s.at[b, j, h], s2_ss.at[(b * 4 + j) * 2 + h])

        @pl.loop(0, 3)
        def _(j):
            for h in (0, 1):
                left(s3s.at[b, j, h], s3_ss.at[(b * 3 + j) * 2 + h])


def fused(tokens, expert_ids, combine_weights, w_gate, w_up, w_down):
    tok_rows, width = tokens.shape
    model = w_gate.shape[1]
    hidden = w_gate.shape[2]
    total = 2 * tok_rows
    half = tok_rows // 4
    vm = pl.BlockSpec(memory_space=pltpu.VMEM)
    hbm = pl.BlockSpec(memory_space=pl.ANY)
    dma = lambda n: pltpu.SemaphoreType.DMA((n,))
    return pl.pallas_call(
        kernel,
        out_shape=jax.ShapeDtypeStruct((tok_rows, width), BF16),
        in_specs=[vm, vm, vm, hbm, hbm, hbm],
        out_specs=vm,
        scratch_shapes=[
            pltpu.VMEM((2, total, model), BF16),
            pltpu.VMEM((2, total, hidden), BF16),
            pltpu.VMEM((model, hidden), BF16),
            pltpu.VMEM((model, hidden), BF16),
            pltpu.VMEM((hidden, model), BF16),
            pltpu.VMEM((4, 8, tok_rows), F32),
            pltpu.VMEM((2, total, 128), F32),
            pltpu.VMEM((2, 4, total, width), F32),
            pltpu.VMEM((2, 4, total, width), BF16),
            pltpu.VMEM((2, 4, 2, 2, half, width), BF16),
            pltpu.VMEM((2, 4, 2, 2, half, width), BF16),
            pltpu.VMEM((2, 4, 2, half, width), BF16),
            pltpu.VMEM((2, 4, 2, half, width), BF16),
            pltpu.VMEM((2, 3, 2, half, width), BF16),
            pltpu.VMEM((2, 3, 2, half, width), BF16),
            dma(3),
            dma(4),
            dma(16), dma(16), dma(16), dma(16), dma(16), dma(16), dma(16), dma(16), dma(16), dma(16),
            dma(4), dma(4), dma(8), dma(8), dma(16), dma(16), dma(16), dma(16), dma(12), dma(12),
        ],
        compiler_params=pltpu.CompilerParams(
            collective_id=0, has_side_effects=True, vmem_limit_bytes=63 * 1024 * 1024
        ),
        cost_estimate=pl.CostEstimate(
            flops=12 * total * model * hidden,
            bytes_accessed=6 * model * hidden,
            transcendentals=2 * total * hidden,
        ),
    )(tokens, expert_ids.T, combine_weights.T, w_gate, w_up, w_down)


def shards(tokens, expert_ids, combine_weights, w_gate, w_up, w_down):
    groups = lax.axis_size("ep")
    tok_rows = tokens.shape[0]
    width_local = tokens.shape[1]
    capacity = min(tok_rows, 4 * tok_rows // groups)
    experts_all = groups * w_gate.shape[0]
    chosen = expert_ids.reshape(-1)
    expert_lane = jnp.arange(experts_all, dtype=jnp.int32)
    onehot = (chosen[:, None] == expert_lane[None, :]).astype(jnp.int32)
    before = jnp.cumsum(onehot, axis=0, dtype=jnp.int32) - onehot
    slot_index = jnp.sum(before * onehot, axis=1)
    position = (chosen * capacity + slot_index).reshape(tok_rows, 2)
    places = jnp.arange(experts_all * capacity, dtype=jnp.int32)
    select = position[:, :, None] == places[None, None, :]
    dispatch = jnp.sum(select.astype(jnp.float32), axis=1).astype(jnp.bfloat16)
    packed = lax.dot_general(
        dispatch, tokens, (((0,), (0,)), ((), ())), preferred_element_type=jnp.float32
    )
    packed = packed.astype(jnp.bfloat16).reshape(experts_all, capacity, width_local)
    arrived = lax.all_to_all(packed, "ep", split_axis=0, concat_axis=0, tiled=True)
    expert_rows = arrived.reshape(groups * capacity, width_local)
    gate_local = w_gate[0]
    up_local = w_up[0]
    down_local = w_down[0]
    section = lax.all_gather(expert_rows, "fsdp", axis=1, tiled=True)
    gate_sums = jnp.dot(section, gate_local, preferred_element_type=jnp.float32)
    up_sums = jnp.dot(section, up_local, preferred_element_type=jnp.float32)
    hidden = (jax.nn.silu(gate_sums) * up_sums).astype(jnp.bfloat16)
    summed = lax.psum_scatter(
        lax.dot_general(
            down_local, hidden, (((0,), (1,)), ((), ())), preferred_element_type=jnp.float32
        ),
        "fsdp",
        scatter_dimension=0,
        tiled=True,
    )
    result = summed.T.astype(jnp.bfloat16)
    returned = lax.all_to_all(
        result.reshape(groups, capacity, width_local), "ep", split_axis=0, concat_axis=0, tiled=True
    )
    weighting = jnp.sum(jnp.where(select, combine_weights[:, :, None], 0.0), axis=1)
    mixed_rows = jnp.dot(
        weighting,
        returned.reshape(-1, width_local).astype(jnp.float32),
        precision=lax.Precision.HIGHEST,
    )
    return mixed_rows.astype(jnp.bfloat16)


def solution(mesh):
    in_specs = (
        P("ep", "fsdp"),
        P("ep", None),
        P("ep", None),
        P("ep", None, "fsdp"),
        P("ep", None, "fsdp"),
        P("ep", "fsdp", None),
    )
    out_specs = P("ep", "fsdp")

    def layer(tokens, *rest):
        small = mesh.shape["ep"] == 4 and mesh.shape["fsdp"] == 8
        return (fused if small else shards)(tokens, *rest)

    return jax.shard_map(layer, mesh=mesh, in_specs=in_specs, out_specs=out_specs, check_vma=False)
```

```python
import jax
import jax.numpy as jnp
from jax import lax
from jax.experimental import pallas as pl
from jax.experimental.pallas import tpu as pltpu
from jax.sharding import PartitionSpec as P

MESH = pl.DeviceIdType.MESH
BF16 = jnp.bfloat16
F32 = jnp.float32


def kernel(
    tok, ids, wts, wg, wu, wd, out,
    rows_all, hid, wgu_v, wd_v, wt, wcol, acc,
    sib_r, s1s, s1r, s2s, s2r, s3s, s3r,
    load_sem, own_sem, z_ss, z_rs, h1_ss, h1_rs, h2_ss, h2_rs, c0_ss, c0_rs, c1_ss, c1_rs,
    wt_send, wt_recv, sib_ss, sib_rs, s1_ss, s1_rs, s2_ss, s2_rs, s3_ss, s3_rs,
):
    tok_rows, width = tok.shape
    part = tok_rows // 2
    half = tok_rows // 4
    ep = lax.axis_index("ep")
    fs = lax.axis_index("fsdp")
    y, x = ep // 2, ep % 2
    z, c = fs // 2, fs % 2
    group = [ep, ep + 1 - 2 * x, ep + 2 - 4 * y, 3 - ep]

    def sec(k, plane):
        core = c if plane == 0 else 1 - c
        return ((z + k) % 4) * 2 + core

    sib = (ep, z * 2 + 1 - c)
    x_nbr, y_nbr, diag = (group[1], fs), (group[2], fs), (group[3], fs)
    z_dev = [None] + [(ep, sec(k, 0)) for k in (1, 2, 3)]

    tile = hid.shape[2] // 4
    up_loads, down_loads = [], []
    for i in range(4):
        for m, w in ((0, wg), (1, wu)):
            up_loads.append(pltpu.make_async_copy(
                w.at[0, :, pl.ds(i * tile, tile)],
                wgu_v.at[:, pl.ds((i * 2 + m) * tile, tile)],
                load_sem.at[i * 2 + m],
            ))
        for m, plane in ((0, 1), (1, 0)):
            at = pl.ds(pl.multiple_of(sec((i + 1) % 4, plane) * width, 128), width)
            down_loads.append(pltpu.make_async_copy(
                wd.at[0, :, at],
                wd_v.at[:, pl.ds((i * 2 + m) * width, width)],
                load_sem.at[8 + i * 2 + m],
            ))

    def place(r, h):
        gy = y if r < 2 else 1 - y
        gx = x if r % 2 == 0 else 1 - x
        return gy * 2 + gx if h == 0 else gx * 2 + gy

    def grows(r, h):
        return pl.ds(pl.multiple_of(h * part * 2 + place(r, h) * half, half), half)

    def prows(h, other):
        first = y if h == 0 else x
        if other:
            first = 1 - first
        return pl.ds(pl.multiple_of(h * part * 2 + first * part, part), part)

    def cols(s):
        return pl.ds(pl.multiple_of(s * width, 128), width)

    def own_block(b, h, k):
        return rows_all.at[b, grows(0, h), cols(sec(k, 0))]

    def pair(b, h, k, other, plane=0):
        return rows_all.at[b, prows(h, other), cols(sec(k, plane))]

    def tok_part(b, h):
        return tok.at[pl.ds(b * part + h * half, half)]

    both = [(b, h) for b in (0, 1) for h in (0, 1)]
    own = [
        pltpu.make_async_copy(tok_part(b, h), own_block(b, h, 0), own_sem.at[b * 2 + h])
        for b, h in both
    ]
    for d in own:
        d.start()

    lane_e = lax.broadcasted_iota(jnp.int32, (8, tok_rows), 0)
    wt[0] = jnp.where(ids[0:1, :] == lane_e, wts[0:1, :], 0.0) + jnp.where(
        ids[1:2, :] == lane_e, wts[1:2, :], 0.0
    )

    barrier = pltpu.get_barrier_semaphore()
    partners = [sib, x_nbr, y_nbr, diag, z_dev[1], z_dev[2], z_dev[3]]
    for dev in partners:
        pl.semaphore_signal(barrier, inc=1, device_id=dev, device_id_type=MESH)
    for d in up_loads:
        d.start()
    for d in own:
        d.wait()
    pl.semaphore_wait(barrier, len(partners))

    def rcopy(src, dst, ss, rs, dev):
        return pltpu.make_async_remote_copy(
            src_ref=src, dst_ref=dst, send_sem=ss, recv_sem=rs, device_id=dev, device_id_type=MESH
        )

    def send(src, dst, ss, rs, dev):
        rcopy(src, dst, ss, rs, dev).start()

    def took(dst, rs):
        rcopy(dst, dst, z_ss.at[0], rs, sib).wait_recv()

    def left(src, ss):
        rcopy(src, src, ss, z_rs.at[0], sib).wait_send()

    def num(b, h, k):
        return (b * 2 + h) * 4 + k

    def own_z(b):
        for h in (0, 1):
            for k in (1, 2, 3):
                send(tok_part(b, h), own_block(b, h, 0), z_ss.at[num(b, h, k)],
                     z_rs.at[num(b, h, 4 - k)], z_dev[k])

    def first(b, k):
        for h, dev in ((0, x_nbr), (1, y_nbr)):
            n = num(b, h, k)
            at = own_block(b, h, k)
            if k != 0:
                took(at, z_rs.at[n])
            send(at, at, h1_ss.at[n], h1_rs.at[n], dev)

    def second(b, k):
        for h, r, dev in ((0, 1, y_nbr), (1, 2, x_nbr)):
            n = num(b, h, k)
            took(rows_all.at[b, grows(r, h), cols(sec(k, 0))], h1_rs.at[n])
            at = pair(b, h, k, False)
            send(at, at, h2_ss.at[n], h2_rs.at[n], dev)
            send(at, at, c0_ss.at[n], c0_rs.at[n], sib)

    def last(b, k):
        for h in (0, 1):
            n = num(b, h, k)
            at = pair(b, h, k, True)
            took(at, h2_rs.at[n])
            send(at, at, c1_ss.at[n], c1_rs.at[n], sib)

    def gathered(b):
        @pl.loop(0, 4)
        def _(k):
            for h in (0, 1):
                took(pair(b, h, k, False, 1), c0_rs.at[num(b, h, k)])
                took(pair(b, h, k, True, 1), c1_rs.at[num(b, h, k)])

    def all_sent(b):
        @pl.loop(0, 4)
        def _(k):
            for h in (0, 1):
                n = num(b, h, k)
                left(own_block(b, h, k), h1_ss.at[n])
                left(pair(b, h, k, False), h2_ss.at[n])
                left(pair(b, h, k, False), c0_ss.at[n])
                left(pair(b, h, k, True), c1_ss.at[n])

        for h in (0, 1):
            for k in (1, 2, 3):
                left(tok_part(b, h), z_ss.at[num(b, h, k)])

    own_z(0)
    first(0, 0)
    for i, dev in ((1, x_nbr), (2, y_nbr), (3, diag)):
        send(wt.at[0], wt.at[i], wt_send.at[i], wt_recv.at[i], dev)
    for d in down_loads:
        d.start()
    second(0, 0)
    first(0, 1)
    first(0, 3)
    first(0, 2)
    own_z(1)
    first(1, 0)
    second(0, 1)
    second(0, 3)
    second(0, 2)

    eye = lax.broadcasted_iota(jnp.int32, (tok_rows, tok_rows), 0) == lax.broadcasted_iota(
        jnp.int32, (tok_rows, tok_rows), 1
    )
    for r in range(4):
        if r > 0:
            took(wt.at[r], wt_recv.at[r])
        row = jnp.sum(jnp.where(lane_e == ep, wt[r], 0.0), axis=0, keepdims=True)
        col = jnp.sum(jnp.where(eye, row, 0.0), axis=1, keepdims=True)
        for b, h in both:
            lo = b * part + h * half
            wcol[b, grows(r, h), :] = jnp.broadcast_to(col[lo:lo + half], (half, 128))

    for k in (0, 1, 3, 2):
        last(0, k)
    for k in (1, 3, 2):
        first(1, k)

    def up(b, i):
        at = pl.ds(pl.multiple_of(i * 2 * tile, tile), 2 * tile)
        gu = jnp.dot(rows_all[b], wgu_v[:, at], preferred_element_type=F32)
        g, u = gu[:, :tile], gu[:, tile:]
        hid[b, :, pl.ds(pl.multiple_of(i * tile, tile), tile)] = (
            g / (1.0 + jnp.exp(-g)) * u
        ).astype(BF16)

    def stage0(b, j):
        s = cols(sec((j + 1) % 4, 1))
        n = b * 4 + j
        at = pl.ds(pl.multiple_of(j * 2 * width, 128), 2 * width)
        p = jnp.dot(hid[b], wd_v[:, at], preferred_element_type=F32)
        scale = wcol[b, :, 0:1]
        rows_all[b, :, s] = (p[:, :width] * scale).astype(BF16)
        send(rows_all.at[b, :, s], sib_r.at[b, j], sib_ss.at[n], sib_rs.at[n], sib)
        acc[b, j] = p[:, width:] * scale

    def stage1(b, j):
        took(sib_r.at[b, j], sib_rs.at[b * 4 + j])
        for h, gone, dev in ((0, (2, 3), y_nbr), (1, (1, 3), x_nbr)):
            n = (b * 4 + j) * 2 + h
            for i, r in enumerate(gone):
                at = grows(r, h)
                s1s[b, j, h, i] = (acc[b, j, at, :] + sib_r[b, j, at, :].astype(F32)).astype(BF16)
            send(s1s.at[b, j, h], s1r.at[b, j, h], s1_ss.at[n], s1_rs.at[n], dev)
        for h, kept in ((0, (0, 1)), (1, (0, 2))):
            for r in kept:
                at = grows(r, h)
                acc[b, j, at, :] = acc[b, j, at, :] + sib_r[b, j, at, :].astype(F32)

    def stage2(b, j):
        for h, r, dev in ((0, 1, x_nbr), (1, 2, y_nbr)):
            n = (b * 4 + j) * 2 + h
            took(s1r.at[b, j, h], s1_rs.at[n])
            s2s[b, j, h] = (acc[b, j, grows(r, h), :] + s1r[b, j, h, 1].astype(F32)).astype(BF16)
            send(s2s.at[b, j, h], s2r.at[b, j, h], s2_ss.at[n], s2_rs.at[n], dev)

    def summed(b, j, h):
        took(s2r.at[b, j, h], s2_rs.at[(b * 4 + j) * 2 + h])
        return acc[b, j, grows(0, h), :] + s1r[b, j, h, 0].astype(F32) + s2r[b, j, h].astype(F32)

    def stage3(b, j):
        for h in (0, 1):
            n = (b * 3 + j) * 2 + h
            s3s[b, j, h] = summed(b, j, h).astype(BF16)
            send(s3s.at[b, j, h], s3r.at[b, j, h], s3_ss.at[n], s3_rs.at[n], (ep, sec(j + 1, 0)))

    def finish(b):
        for h in (0, 1):
            v = summed(b, 3, h)
            for i in range(3):
                took(s3r.at[b, i, h], s3_rs.at[(b * 3 + i) * 2 + h])
                v = v + s3r[b, i, h].astype(F32)
            out[pl.ds(b * part + h * half, half), :] = v.astype(BF16)

    gathered(0)
    for d in up_loads:
        d.wait()

    @pl.loop(0, 4)
    def _(i):
        up(0, i)
        second(1, i)

    all_sent(0)
    for d in down_loads:
        d.wait()

    @pl.loop(0, 4)
    def _(j):
        stage0(0, j)
        last(1, j)

        @pl.when(j > 0)
        def _():
            stage1(0, j - 1)

    stage1(0, 3)
    gathered(1)

    @pl.loop(0, 4)
    def _(i):
        up(1, i)
        stage2(0, i)

        @pl.when(i > 0)
        def _():
            stage3(0, i - 1)

    all_sent(1)

    @pl.loop(0, 4)
    def _(j):
        stage0(1, j)

        @pl.when(j > 0)
        def _():
            stage1(1, j - 1)

        @pl.when(j > 1)
        def _():
            stage2(1, j - 2)

    stage1(1, 3)
    stage2(1, 2)
    stage3(1, 0)
    finish(0)
    stage3(1, 1)
    stage2(1, 3)
    stage3(1, 2)
    finish(1)

    for i in (1, 2, 3):
        left(wt.at[0], wt_send.at[i])
    for b in (0, 1):
        @pl.loop(0, 4)
        def _(j):
            left(sib_r.at[b, j], sib_ss.at[b * 4 + j])
            for h in (0, 1):
                left(s1s.at[b, j, h], s1_ss.at[(b * 4 + j) * 2 + h])
                left(s2s.at[b, j, h], s2_ss.at[(b * 4 + j) * 2 + h])

        @pl.loop(0, 3)
        def _(j):
            for h in (0, 1):
                left(s3s.at[b, j, h], s3_ss.at[(b * 3 + j) * 2 + h])


def fused(tokens, expert_ids, combine_weights, w_gate, w_up, w_down):
    tok_rows, width = tokens.shape
    model = w_gate.shape[1]
    hidden = w_gate.shape[2]
    total = 2 * tok_rows
    half = tok_rows // 4
    vm = pl.BlockSpec(memory_space=pltpu.VMEM)
    hbm = pl.BlockSpec(memory_space=pl.ANY)
    dma = lambda n: pltpu.SemaphoreType.DMA((n,))
    return pl.pallas_call(
        kernel,
        out_shape=jax.ShapeDtypeStruct((tok_rows, width), BF16),
        in_specs=[vm, vm, vm, hbm, hbm, hbm],
        out_specs=vm,
        scratch_shapes=[
            pltpu.VMEM((2, total, model), BF16),
            pltpu.VMEM((2, total, hidden), BF16),
            pltpu.VMEM((model, 2 * hidden), BF16),
            pltpu.VMEM((hidden, model), BF16),
            pltpu.VMEM((4, 8, tok_rows), F32),
            pltpu.VMEM((2, total, 128), F32),
            pltpu.VMEM((2, 4, total, width), F32),
            pltpu.VMEM((2, 4, total, width), BF16),
            pltpu.VMEM((2, 4, 2, 2, half, width), BF16),
            pltpu.VMEM((2, 4, 2, 2, half, width), BF16),
            pltpu.VMEM((2, 4, 2, half, width), BF16),
            pltpu.VMEM((2, 4, 2, half, width), BF16),
            pltpu.VMEM((2, 3, 2, half, width), BF16),
            pltpu.VMEM((2, 3, 2, half, width), BF16),
            dma(16),
            dma(4),
            dma(16), dma(16), dma(16), dma(16), dma(16), dma(16), dma(16), dma(16), dma(16), dma(16),
            dma(4), dma(4), dma(8), dma(8), dma(16), dma(16), dma(16), dma(16), dma(12), dma(12),
        ],
        compiler_params=pltpu.CompilerParams(
            collective_id=0, has_side_effects=True, vmem_limit_bytes=63 * 1024 * 1024
        ),
        cost_estimate=pl.CostEstimate(
            flops=12 * total * model * hidden,
            bytes_accessed=6 * model * hidden,
            transcendentals=2 * total * hidden,
        ),
    )(tokens, expert_ids.T, combine_weights.T, w_gate, w_up, w_down)


def shards(tokens, expert_ids, combine_weights, w_gate, w_up, w_down):
    groups = lax.axis_size("ep")
    tok_rows = tokens.shape[0]
    width_local = tokens.shape[1]
    capacity = min(tok_rows, 4 * tok_rows // groups)
    experts_all = groups * w_gate.shape[0]
    chosen = expert_ids.reshape(-1)
    expert_lane = jnp.arange(experts_all, dtype=jnp.int32)
    onehot = (chosen[:, None] == expert_lane[None, :]).astype(jnp.int32)
    before = jnp.cumsum(onehot, axis=0, dtype=jnp.int32) - onehot
    slot_index = jnp.sum(before * onehot, axis=1)
    position = (chosen * capacity + slot_index).reshape(tok_rows, 2)
    places = jnp.arange(experts_all * capacity, dtype=jnp.int32)
    select = position[:, :, None] == places[None, None, :]
    dispatch = jnp.sum(select.astype(jnp.float32), axis=1).astype(jnp.bfloat16)
    packed = lax.dot_general(
        dispatch, tokens, (((0,), (0,)), ((), ())), preferred_element_type=jnp.float32
    )
    packed = packed.astype(jnp.bfloat16).reshape(experts_all, capacity, width_local)
    arrived = lax.all_to_all(packed, "ep", split_axis=0, concat_axis=0, tiled=True)
    expert_rows = arrived.reshape(groups * capacity, width_local)
    gate_local = w_gate[0]
    up_local = w_up[0]
    down_local = w_down[0]
    section = lax.all_gather(expert_rows, "fsdp", axis=1, tiled=True)
    gate_sums = jnp.dot(section, gate_local, preferred_element_type=jnp.float32)
    up_sums = jnp.dot(section, up_local, preferred_element_type=jnp.float32)
    hidden = (jax.nn.silu(gate_sums) * up_sums).astype(jnp.bfloat16)
    summed = lax.psum_scatter(
        lax.dot_general(
            down_local, hidden, (((0,), (1,)), ((), ())), preferred_element_type=jnp.float32
        ),
        "fsdp",
        scatter_dimension=0,
        tiled=True,
    )
    result = summed.T.astype(jnp.bfloat16)
    returned = lax.all_to_all(
        result.reshape(groups, capacity, width_local), "ep", split_axis=0, concat_axis=0, tiled=True
    )
    weighting = jnp.sum(jnp.where(select, combine_weights[:, :, None], 0.0), axis=1)
    mixed_rows = jnp.dot(
        weighting,
        returned.reshape(-1, width_local).astype(jnp.float32),
        precision=lax.Precision.HIGHEST,
    )
    return mixed_rows.astype(jnp.bfloat16)


def solution(mesh):
    in_specs = (
        P("ep", "fsdp"),
        P("ep", None),
        P("ep", None),
        P("ep", None, "fsdp"),
        P("ep", None, "fsdp"),
        P("ep", "fsdp", None),
    )
    out_specs = P("ep", "fsdp")

    def layer(tokens, *rest):
        small = mesh.shape["ep"] == 4 and mesh.shape["fsdp"] == 8
        return (fused if small else shards)(tokens, *rest)

    return jax.shard_map(layer, mesh=mesh, in_specs=in_specs, out_specs=out_specs, check_vma=False)
```

```python
import jax
import jax.numpy as jnp
from jax import lax
from jax.experimental import pallas as pl
from jax.experimental.pallas import tpu as pltpu
from jax.sharding import PartitionSpec as P

MESH = pl.DeviceIdType.MESH
BF16 = jnp.bfloat16
F32 = jnp.float32


def kernel(
    tok, ids, wts, wg, wu, wd, out,
    rows_all, hid, wgu_v, wd_v, wt, wcol, acc,
    sib_r, s1s, s1r, s2s, s2r, s3s, s3r,
    load_sem, own_sem, z_ss, z_rs, h1_ss, h1_rs, h2_ss, h2_rs, c0_ss, c0_rs, c1_ss, c1_rs,
    wt_send, wt_recv, sib_ss, sib_rs, s1_ss, s1_rs, s2_ss, s2_rs, s3_ss, s3_rs,
):
    tok_rows, width = tok.shape
    part = tok_rows
    half = tok_rows // 2
    ep = lax.axis_index("ep")
    fs = lax.axis_index("fsdp")
    y, x = ep // 2, ep % 2
    z, c = fs // 2, fs % 2
    group = [ep, ep + 1 - 2 * x, ep + 2 - 4 * y, 3 - ep]

    def sec(k, plane):
        core = c if plane == 0 else 1 - c
        return ((z + k) % 4) * 2 + core

    sib = (ep, z * 2 + 1 - c)
    x_nbr, y_nbr, diag = (group[1], fs), (group[2], fs), (group[3], fs)
    z_dev = [None] + [(ep, sec(k, 0)) for k in (1, 2, 3)]

    tile = hid.shape[2] // 4
    up_loads, down_loads = [], []
    for i in range(4):
        for m, w in ((0, wg), (1, wu)):
            up_loads.append(pltpu.make_async_copy(
                w.at[0, :, pl.ds(i * tile, tile)],
                wgu_v.at[:, pl.ds((i * 2 + m) * tile, tile)],
                load_sem.at[i * 2 + m],
            ))
        for m, plane in ((0, 1), (1, 0)):
            at = pl.ds(pl.multiple_of(sec((i + 1) % 4, plane) * width, 128), width)
            down_loads.append(pltpu.make_async_copy(
                wd.at[0, :, at],
                wd_v.at[:, pl.ds((i * 2 + m) * width, width)],
                load_sem.at[8 + i * 2 + m],
            ))

    def place(r, h):
        gy = y if r < 2 else 1 - y
        gx = x if r % 2 == 0 else 1 - x
        return gy * 2 + gx if h == 0 else gx * 2 + gy

    def grows(r, h):
        return pl.ds(pl.multiple_of(h * part * 2 + place(r, h) * half, half), half)

    def prows(h, other):
        first = y if h == 0 else x
        if other:
            first = 1 - first
        return pl.ds(pl.multiple_of(h * part * 2 + first * part, part), part)

    def cols(s):
        return pl.ds(pl.multiple_of(s * width, 128), width)

    def own_block(b, h, k):
        return rows_all.at[b, grows(0, h), cols(sec(k, 0))]

    def pair(b, h, k, other, plane=0):
        return rows_all.at[b, prows(h, other), cols(sec(k, plane))]

    def tok_part(b, h):
        return tok.at[pl.ds(b * part + h * half, half)]

    both = [(0, 0), (0, 1)]
    own = [
        pltpu.make_async_copy(tok_part(b, h), own_block(b, h, 0), own_sem.at[b * 2 + h])
        for b, h in both
    ]
    for d in own:
        d.start()

    lane_e = lax.broadcasted_iota(jnp.int32, (8, tok_rows), 0)
    wt[0] = jnp.where(ids[0:1, :] == lane_e, wts[0:1, :], 0.0) + jnp.where(
        ids[1:2, :] == lane_e, wts[1:2, :], 0.0
    )

    barrier = pltpu.get_barrier_semaphore()
    partners = [sib, x_nbr, y_nbr, diag, z_dev[1], z_dev[2], z_dev[3]]
    for dev in partners:
        pl.semaphore_signal(barrier, inc=1, device_id=dev, device_id_type=MESH)
    for d in up_loads:
        d.start()
    for d in own:
        d.wait()
    pl.semaphore_wait(barrier, len(partners))

    def rcopy(src, dst, ss, rs, dev):
        return pltpu.make_async_remote_copy(
            src_ref=src, dst_ref=dst, send_sem=ss, recv_sem=rs, device_id=dev, device_id_type=MESH
        )

    def send(src, dst, ss, rs, dev):
        rcopy(src, dst, ss, rs, dev).start()

    def took(dst, rs):
        rcopy(dst, dst, z_ss.at[0], rs, sib).wait_recv()

    def left(src, ss):
        rcopy(src, src, ss, z_rs.at[0], sib).wait_send()

    def num(b, h, k):
        return (b * 2 + h) * 4 + k

    def own_z(b):
        for h in (0, 1):
            for k in (1, 2, 3):
                send(tok_part(b, h), own_block(b, h, 0), z_ss.at[num(b, h, k)],
                     z_rs.at[num(b, h, 4 - k)], z_dev[k])

    def first(b, k):
        for h, dev in ((0, x_nbr), (1, y_nbr)):
            n = num(b, h, k)
            at = own_block(b, h, k)
            if k != 0:
                took(at, z_rs.at[n])
            send(at, at, h1_ss.at[n], h1_rs.at[n], dev)

    def second(b, k):
        for h, r, dev in ((0, 1, y_nbr), (1, 2, x_nbr)):
            n = num(b, h, k)
            took(rows_all.at[b, grows(r, h), cols(sec(k, 0))], h1_rs.at[n])
            at = pair(b, h, k, False)
            send(at, at, h2_ss.at[n], h2_rs.at[n], dev)
            send(at, at, c0_ss.at[n], c0_rs.at[n], sib)

    def last(b, k):
        for h in (0, 1):
            n = num(b, h, k)
            at = pair(b, h, k, True)
            took(at, h2_rs.at[n])
            send(at, at, c1_ss.at[n], c1_rs.at[n], sib)

    def gathered(b, k):
        for h in (0, 1):
            took(pair(b, h, k, False, 1), c0_rs.at[num(b, h, k)])
            took(pair(b, h, k, True, 1), c1_rs.at[num(b, h, k)])

    def all_sent(b):
        @pl.loop(0, 4)
        def _(k):
            for h in (0, 1):
                n = num(b, h, k)
                left(own_block(b, h, k), h1_ss.at[n])
                left(pair(b, h, k, False), h2_ss.at[n])
                left(pair(b, h, k, False), c0_ss.at[n])
                left(pair(b, h, k, True), c1_ss.at[n])

        for h in (0, 1):
            for k in (1, 2, 3):
                left(tok_part(b, h), z_ss.at[num(b, h, k)])

    own_z(0)
    first(0, 0)
    for i, dev in ((1, x_nbr), (2, y_nbr), (3, diag)):
        send(wt.at[0], wt.at[i], wt_send.at[i], wt_recv.at[i], dev)
    second(0, 0)
    first(0, 1)
    for d in down_loads:
        d.start()

    eye = lax.broadcasted_iota(jnp.int32, (tok_rows, tok_rows), 0) == lax.broadcasted_iota(
        jnp.int32, (tok_rows, tok_rows), 1
    )
    for r in range(4):
        if r > 0:
            took(wt.at[r], wt_recv.at[r])
        row = jnp.sum(jnp.where(lane_e == ep, wt[r], 0.0), axis=0, keepdims=True)
        col = jnp.sum(jnp.where(eye, row, 0.0), axis=1, keepdims=True)
        for b, h in both:
            lo = b * part + h * half
            wcol[b, grows(r, h), :] = jnp.broadcast_to(col[lo:lo + half], (half, 128))

    def up(k, i, begin, end):
        rows = pl.ds(pl.multiple_of(((z + k) % 4) * 2 * width, 128), 2 * width)
        at = pl.ds(pl.multiple_of(i * 2 * tile, tile), 2 * tile)
        gu = jnp.dot(rows_all[0, :, rows], wgu_v[rows, at], preferred_element_type=F32)
        if not begin:
            gu = gu + acc[0, i, :, 0:2 * tile]
        if not end:
            acc[0, i, :, 0:2 * tile] = gu
        else:
            g, u = gu[:, :tile], gu[:, tile:]
            hid[0, :, pl.ds(pl.multiple_of(i * tile, tile), tile)] = (
                g / (1.0 + jnp.exp(-g)) * u
            ).astype(BF16)

    def ups(k, lo, begin=False, end=False):
        @pl.loop(lo, 4)
        def _(i):
            up(k, i, begin, end)

    def stage0(b, j):
        s = cols(sec((j + 1) % 4, 1))
        n = b * 4 + j

        def down(m):
            at = pl.ds(pl.multiple_of((j * 2 + m) * width, 128), width)
            p = jnp.dot(hid[b], wd_v[:, at], preferred_element_type=F32)
            return p * wcol[b, :, 0:1]

        rows_all[b, :, s] = down(0).astype(BF16)
        send(rows_all.at[b, :, s], sib_r.at[b, j], sib_ss.at[n], sib_rs.at[n], sib)
        acc[b, j] = down(1)

    def stage1(b, j):
        took(sib_r.at[b, j], sib_rs.at[b * 4 + j])
        for h, gone, dev in ((0, (2, 3), y_nbr), (1, (1, 3), x_nbr)):
            n = (b * 4 + j) * 2 + h
            for i, r in enumerate(gone):
                at = grows(r, h)
                s1s[b, j, h, i] = (acc[b, j, at, :] + sib_r[b, j, at, :].astype(F32)).astype(BF16)
            send(s1s.at[b, j, h], s1r.at[b, j, h], s1_ss.at[n], s1_rs.at[n], dev)
        for h, kept in ((0, (0, 1)), (1, (0, 2))):
            for r in kept:
                at = grows(r, h)
                acc[b, j, at, :] = acc[b, j, at, :] + sib_r[b, j, at, :].astype(F32)

    def stage2(b, j):
        for h, r, dev in ((0, 1, x_nbr), (1, 2, y_nbr)):
            n = (b * 4 + j) * 2 + h
            took(s1r.at[b, j, h], s1_rs.at[n])
            s2s[b, j, h] = (acc[b, j, grows(r, h), :] + s1r[b, j, h, 1].astype(F32)).astype(BF16)
            send(s2s.at[b, j, h], s2r.at[b, j, h], s2_ss.at[n], s2_rs.at[n], dev)

    def summed(b, j, h):
        took(s2r.at[b, j, h], s2_rs.at[(b * 4 + j) * 2 + h])
        return acc[b, j, grows(0, h), :] + s1r[b, j, h, 0].astype(F32) + s2r[b, j, h].astype(F32)

    def stage3(b, j):
        for h in (0, 1):
            n = (b * 3 + j) * 2 + h
            s3s[b, j, h] = summed(b, j, h).astype(BF16)
            send(s3s.at[b, j, h], s3r.at[b, j, h], s3_ss.at[n], s3_rs.at[n], (ep, sec(j + 1, 0)))

    def finish(b):
        for h in (0, 1):
            v = summed(b, 3, h)
            for i in range(3):
                took(s3r.at[b, i, h], s3_rs.at[(b * 3 + i) * 2 + h])
                v = v + s3r[b, i, h].astype(F32)
            out[pl.ds(b * part + h * half, half), :] = v.astype(BF16)

    last(0, 0)
    second(0, 1)
    first(0, 3)
    first(0, 2)
    gathered(0, 0)
    for d in up_loads:
        d.wait()
    ups(0, 0, begin=True)
    last(0, 1)
    second(0, 3)
    gathered(0, 1)
    up(1, 0, False, False)
    second(0, 2)
    ups(1, 1)
    last(0, 3)
    gathered(0, 3)
    ups(3, 0)
    last(0, 2)
    gathered(0, 2)
    ups(2, 0, end=True)
    all_sent(0)
    for d in down_loads:
        d.wait()

    @pl.loop(0, 4)
    def _(j):
        stage0(0, j)
        stage1(0, j)

        @pl.when(j > 0)
        def _():
            stage2(0, j - 1)

        @pl.when(j > 1)
        def _():
            stage3(0, j - 2)

    stage2(0, 3)
    stage3(0, 2)
    finish(0)

    for i in (1, 2, 3):
        left(wt.at[0], wt_send.at[i])
    for b in (0,):
        @pl.loop(0, 4)
        def _(j):
            left(sib_r.at[b, j], sib_ss.at[b * 4 + j])
            for h in (0, 1):
                left(s1s.at[b, j, h], s1_ss.at[(b * 4 + j) * 2 + h])
                left(s2s.at[b, j, h], s2_ss.at[(b * 4 + j) * 2 + h])

        @pl.loop(0, 3)
        def _(j):
            for h in (0, 1):
                left(s3s.at[b, j, h], s3_ss.at[(b * 3 + j) * 2 + h])


def fused(tokens, expert_ids, combine_weights, w_gate, w_up, w_down):
    tok_rows, width = tokens.shape
    model = w_gate.shape[1]
    hidden = w_gate.shape[2]
    total = 4 * tok_rows
    half = tok_rows // 2
    vm = pl.BlockSpec(memory_space=pltpu.VMEM)
    hbm = pl.BlockSpec(memory_space=pl.ANY)
    dma = lambda n: pltpu.SemaphoreType.DMA((n,))
    return pl.pallas_call(
        kernel,
        out_shape=jax.ShapeDtypeStruct((tok_rows, width), BF16),
        in_specs=[vm, vm, vm, hbm, hbm, hbm],
        out_specs=vm,
        scratch_shapes=[
            pltpu.VMEM((1, total, model), BF16),
            pltpu.VMEM((1, total, hidden), BF16),
            pltpu.VMEM((model, 2 * hidden), BF16),
            pltpu.VMEM((hidden, model), BF16),
            pltpu.VMEM((4, 8, tok_rows), F32),
            pltpu.VMEM((1, total, 128), F32),
            pltpu.VMEM((1, 4, total, width), F32),
            pltpu.VMEM((1, 4, total, width), BF16),
            pltpu.VMEM((1, 4, 2, 2, half, width), BF16),
            pltpu.VMEM((1, 4, 2, 2, half, width), BF16),
            pltpu.VMEM((1, 4, 2, half, width), BF16),
            pltpu.VMEM((1, 4, 2, half, width), BF16),
            pltpu.VMEM((1, 3, 2, half, width), BF16),
            pltpu.VMEM((1, 3, 2, half, width), BF16),
            dma(16),
            dma(2),
            dma(8), dma(8), dma(8), dma(8), dma(8), dma(8), dma(8), dma(8), dma(8), dma(8),
            dma(4), dma(4), dma(4), dma(4), dma(8), dma(8), dma(8), dma(8), dma(6), dma(6),
        ],
        compiler_params=pltpu.CompilerParams(
            collective_id=0, has_side_effects=True, vmem_limit_bytes=63 * 1024 * 1024
        ),
        cost_estimate=pl.CostEstimate(
            flops=6 * total * model * hidden,
            bytes_accessed=6 * model * hidden,
            transcendentals=total * hidden,
        ),
    )(tokens, expert_ids.T, combine_weights.T, w_gate, w_up, w_down)


def shards(tokens, expert_ids, combine_weights, w_gate, w_up, w_down):
    groups = lax.axis_size("ep")
    tok_rows = tokens.shape[0]
    width_local = tokens.shape[1]
    capacity = min(tok_rows, 4 * tok_rows // groups)
    experts_all = groups * w_gate.shape[0]
    chosen = expert_ids.reshape(-1)
    expert_lane = jnp.arange(experts_all, dtype=jnp.int32)
    onehot = (chosen[:, None] == expert_lane[None, :]).astype(jnp.int32)
    before = jnp.cumsum(onehot, axis=0, dtype=jnp.int32) - onehot
    slot_index = jnp.sum(before * onehot, axis=1)
    position = (chosen * capacity + slot_index).reshape(tok_rows, 2)
    places = jnp.arange(experts_all * capacity, dtype=jnp.int32)
    select = position[:, :, None] == places[None, None, :]
    dispatch = jnp.sum(select.astype(jnp.float32), axis=1).astype(jnp.bfloat16)
    packed = lax.dot_general(
        dispatch, tokens, (((0,), (0,)), ((), ())), preferred_element_type=jnp.float32
    )
    packed = packed.astype(jnp.bfloat16).reshape(experts_all, capacity, width_local)
    arrived = lax.all_to_all(packed, "ep", split_axis=0, concat_axis=0, tiled=True)
    expert_rows = arrived.reshape(groups * capacity, width_local)
    gate_local = w_gate[0]
    up_local = w_up[0]
    down_local = w_down[0]
    section = lax.all_gather(expert_rows, "fsdp", axis=1, tiled=True)
    gate_sums = jnp.dot(section, gate_local, preferred_element_type=jnp.float32)
    up_sums = jnp.dot(section, up_local, preferred_element_type=jnp.float32)
    hidden = (jax.nn.silu(gate_sums) * up_sums).astype(jnp.bfloat16)
    summed = lax.psum_scatter(
        lax.dot_general(
            down_local, hidden, (((0,), (1,)), ((), ())), preferred_element_type=jnp.float32
        ),
        "fsdp",
        scatter_dimension=0,
        tiled=True,
    )
    result = summed.T.astype(jnp.bfloat16)
    returned = lax.all_to_all(
        result.reshape(groups, capacity, width_local), "ep", split_axis=0, concat_axis=0, tiled=True
    )
    weighting = jnp.sum(jnp.where(select, combine_weights[:, :, None], 0.0), axis=1)
    mixed_rows = jnp.dot(
        weighting,
        returned.reshape(-1, width_local).astype(jnp.float32),
        precision=lax.Precision.HIGHEST,
    )
    return mixed_rows.astype(jnp.bfloat16)


def solution(mesh):
    in_specs = (
        P("ep", "fsdp"),
        P("ep", None),
        P("ep", None),
        P("ep", None, "fsdp"),
        P("ep", None, "fsdp"),
        P("ep", "fsdp", None),
    )
    out_specs = P("ep", "fsdp")

    def layer(tokens, *rest):
        small = mesh.shape["ep"] == 4 and mesh.shape["fsdp"] == 8
        return (fused if small else shards)(tokens, *rest)

    return jax.shard_map(layer, mesh=mesh, in_specs=in_specs, out_specs=out_specs, check_vma=False)
```
